512 devices in a mesh: fsdp: 16 (over z_hi, x), ctx: 32 (over z_lo, y, core).
Axes of the slice: x: 4, y: 4, z: 16 (z_hi: 4, z_lo: 4; z = z_hi * 4 + z_lo), core: 2. Of those that a mesh axis runs over, the one named last changes fastest.
Arguments:
- features: bfloat16 [16, 3, 2048, 8192], P('fsdp', None, None, 'ctx'), may hold values from -6 to 6
- short_taps: bfloat16 [7, 3, 2048], replicated, may hold values from -2 to 2
- filters: bfloat16 [128, 128], replicated, may hold values from -0.5 to 0.5
- out_weight: bfloat16 [2048, 2048], P('fsdp'), may hold values from -0.125 to 0.125
Outputs:
- mixed_out: bfloat16 [16, 8192, 2048], P('fsdp', 'ctx')
The draws below stay inside these ranges and needn't reach their ends.
All inputs are finite; a program needn't handle non-finite values.
Results may differ from the reference program's by a relative error of at most 0.0058.
Values may be sent and summed in bfloat16 or wider, within the bound.
A program may use at most 128 MiB of HBM per device.

```python
import jax
import jax.numpy as jnp
from jax import lax

DC = 2048
DOUT = 2048
LF = 128
KS = 7
SEQS = 16
L = 8192
GROUPS = 128


def block_scale(own_key, shape, split, least, top_value):
    gain, own = 1.0, jax.random.fold_in(own_key, 6)
    for dim, parts in split:
        heights = jnp.exp(jax.random.uniform(jax.random.fold_in(own, dim), (parts,), jnp.float32, least / len(split), top_value / len(split)))
        gain = gain * jnp.repeat(heights, shape[dim] // parts).reshape([-1 if axis == dim else 1 for axis in range(len(shape))])
    return gain


def normal_values(own_key, shape, spread, reach, cuts=(), kind=jnp.bfloat16):
    loudness = block_scale(own_key, shape, cuts, -0.22, 0.18) if cuts else 1.0
    values = jax.random.normal(own_key, shape, jnp.float32) * spread * loudness
    return jnp.minimum(jnp.maximum(values, -reach), reach).astype(kind)


def setup_inputs(seed: int = 0) -> dict:
    key_list = jax.random.split(jax.random.key(seed), 5)
    return {
        "features": normal_values(key_list[0], (SEQS, 3, DC, L), 1.0, 6.0, ((0, 16), (3, 32))),
        "short_taps": normal_values(key_list[1], (KS, 3, DC), KS ** -0.5, 2.0),
        "filters": normal_values(key_list[2], (GROUPS, LF), LF ** -0.5, 0.5),
        "out_weight": normal_values(key_list[3], (DC, DOUT), DC ** -0.5, 0.125, ((0, 16),)),
    }


def toeplitz(filters):
    groups = filters.shape[0]
    length = filters.shape[1]
    reverse = jnp.concatenate([filters[:, :1], filters[:, :0:-1]], axis=1)
    tiled = jnp.tile(reverse, (1, 2 * length - 1)).reshape(groups, length, 2 * length - 1)[:, :, :length]
    row_index = lax.broadcasted_iota(jnp.int32, (length, length), 0)
    col_index = lax.broadcasted_iota(jnp.int32, (length, length), 1)
    lower = jnp.where(row_index >= col_index, tiled, jnp.zeros_like(tiled))
    upper = jnp.where(row_index < col_index, tiled, jnp.zeros_like(tiled))
    return lower, upper


def short_conv(padded, weights):
    width = weights.shape[0]
    length = padded.shape[2] - width + 1
    result = weights[0][:, :, None] * padded[:, :, width - 1:width - 1 + length]
    for offset in range(1, width):
        result = result + weights[offset][:, :, None] * padded[:, :, width - 1 - offset:width - 1 - offset + length]
    return result


def block_filter(extended, lower, upper):
    channels = extended.shape[0]
    length = lower.shape[1]
    groups = lower.shape[0]
    blocks = extended.shape[1] // length
    shaped = extended.astype(jnp.float32).reshape(groups, channels // groups, blocks, length)
    result = jnp.einsum("gtu,gcbu->gcbt", lower.astype(jnp.float32), shaped[:, :, 1:], precision=lax.Precision.HIGHEST)
    result = result + jnp.einsum("gtu,gcbu->gcbt", upper.astype(jnp.float32), shaped[:, :, :-1], precision=lax.Precision.HIGHEST)
    return result.reshape(channels, (blocks - 1) * length)


def reference(features, short_taps, filters, out_weight):
    weights = short_taps.astype(jnp.float32)
    lower, upper = toeplitz(filters)

    def single(sequence):
        values = sequence.astype(jnp.float32)
        padded = jnp.pad(values, ((0, 0), (0, 0), (KS - 1, 0)))
        convolved = short_conv(padded, weights)
        product = (convolved[1] * convolved[2]).astype(jnp.bfloat16)
        extended = jnp.pad(product, ((0, 0), (LF, 0)))
        filtered = block_filter(extended, lower, upper)
        gated = (convolved[0] * filtered).astype(jnp.bfloat16)
        projected = lax.dot_general(gated, out_weight, (((0,), (0,)), ((), ())), preferred_element_type=jnp.float32)
        return projected.astype(jnp.bfloat16)

    return lax.map(single, features)
```

```python
import functools

import jax
import jax.numpy as jnp
from jax import lax
from jax.experimental import pallas as pl
from jax.experimental.pallas import tpu as pltpu
from jax.sharding import PartitionSpec as P

MESH = pl.DeviceIdType.MESH
F32, BF16 = jnp.float32, jnp.bfloat16
T = 256
C = 128
TILES = 16
TAPS = 7
LF = 128
VMEM_BYTES = 56 * 1024 * 1024
BATCH = 4

SCHEDULE = (
    ("zdirect",), ("P1", 0), ("A", 0), ("S1", 0), ("zf1",), ("P1", 1), ("A", 1), ("S1", 1), ("W", 2),
    ("P1", 2), ("A", 2), ("zf3",), ("P1", 3), ("S2", 0), ("A", 3), ("S2", 1), ("S1", 2), ("B", 0), ("S1", 3),
    ("B", 1), ("S2", 2), ("B", 2), ("S2", 3), ("B", 3), ("M", 0), ("M", 1), ("M", 2), ("M", 3),
)


def kernel(x_ref, taps_hbm, filt_hbm, w_ref, o_ref,
           taps_ref, filt_ref, buf, xs, xt, wt, fr, toe, zs, qs, head, tail, halo, gs, acc, stage,
           ss, rs, lsem, hs, hr, gsend, grecv, osend, orecv, olocal):
    f = lax.axis_index("fsdp")
    c = lax.axis_index("ctx")
    zh, x = f // 4, f % 4
    zl, y, k = c // 8, (c // 2) % 4, c % 2
    z = zh * 4 + zl

    def at(x, y, z, k):
        return ((z // 4) * 4 + x, ((z % 4) * 4 + y) * 2 + k)

    def xy(dp, ds):
        return at((x + dp + (ds - dp) * k) % 4, (y + ds + (dp - ds) * k) % 4, z, k)

    def zz(d):
        return at(x, y, (z + d + 16) % 16, k)

    sibling = at(x, y, z, 1 - k)
    before, after = (f, (c + 31) % 32), (f, (c + 1) % 32)
    inner = ((zl + 1) // 2) % 2
    edge = inner == 0
    sg = (zl // 3) * 2 - 1
    pair = 1 - 2 * (zl % 2)
    srcd = -pair * (1 + 2 * inner)
    first, last = c == 0, c == 31

    def remote(src, dst, s, r, dev):
        return pltpu.make_async_remote_copy(
            src_ref=src, dst_ref=dst, send_sem=s, recv_sem=r, device_id=dev, device_id_type=MESH
        )

    barrier = pltpu.get_barrier_semaphore()

    def sig(d):
        pl.semaphore_signal(barrier, inc=1, device_id=d, device_id_type=MESH)

    for d in (xy(1, 0), xy(3, 0), xy(2, 0), xy(0, 1), xy(0, 3), zz(pair), zz(srcd), sibling):
        sig(d)
    pl.when(edge)(lambda: sig(zz(5 * sg)))
    pl.when(jnp.logical_not(first))(lambda: sig(before))

    def load(b):
        rows = pl.ds(b * BATCH * C, BATCH * C)
        return pltpu.make_async_copy(x_ref.at[0, :, rows], xs.at[:, rows], lsem.at[b])

    own = pltpu.make_async_copy(
        w_ref.at[:, pl.ds(pl.multiple_of(k * 1024 + y * 256, 256), 256)], buf.at[0, 0, 0], lsem.at[4]
    )
    small = (
        pltpu.make_async_copy(filt_hbm, filt_ref, lsem.at[5]),
        pltpu.make_async_copy(taps_hbm, taps_ref, lsem.at[6]),
    )
    own.start()
    for cp in small:
        cp.start()
    for b in range(4):
        load(b).start()
    for cp in small:
        cp.wait()

    for m in range(3):
        row = taps_ref[m].astype(F32)
        for ct in range(TILES):
            wt[ct, 8 * m : 8 * m + TAPS, :] = row[:, ct * C : (ct + 1) * C]
    r_i = lax.broadcasted_iota(jnp.int32, (LF, LF), 0)
    c_i = lax.broadcasted_iota(jnp.int32, (LF, LF), 1)
    flip = jnp.where((r_i + c_i) % LF == 0, 1.0, 0.0).astype(BF16)
    fr[...] = jnp.dot(filt_ref[...], flip, preferred_element_type=F32)

    def build(ct, _):
        rows = fr[pl.ds(pl.multiple_of(ct * 8, 8), 8), :]
        for g in range(8):
            wide = jnp.broadcast_to(rows[g : g + 1, :], (LF, LF))
            turned = pltpu.roll(wide, 0, 1, stride=1, stride_axis=0)
            toe[ct, :, 256 * g : 256 * g + 128] = jnp.where(r_i < c_i, turned, 0.0).astype(BF16)
            toe[ct, :, 256 * g + 128 : 256 * g + 256] = jnp.where(r_i >= c_i, turned, 0.0).astype(BF16)
        return 0

    lax.fori_loop(0, TILES, build, 0)
    xt[:, 0:16, :] = jnp.zeros((3, 16, C), F32)

    def empty():
        halo[...] = jnp.zeros(halo.shape, BF16)
        zs[:, 0:LF, :] = jnp.zeros((TILES, LF, C), BF16)

    pl.when(first)(empty)
    own.wait()
    pl.semaphore_wait(barrier, 7 + 3 * (1 - inner) + jnp.where(last, 0, 1))

    sent = []
    count = [0] * 4

    def send(src, dst, dev, o):
        cp = remote(buf.at[src], buf.at[dst], ss.at[o, count[o]], rs.at[dst], dev)
        count[o] += 1
        cp.start()
        sent.append(cp)

    def got(slot):
        remote(buf.at[slot], buf.at[slot], ss.at[0, 0], rs.at[slot], sibling).wait_recv()

    far = ((1, 1, 13), (3, 1, 14), (5, 3, 15))

    def zdirect():
        def go():
            for m, o, n in far:
                remote(buf.at[0, 0, 0], buf.at[o, 0, 0], ss.at[0, n], rs.at[o, 0, 0], zz(m * sg)).start()

        pl.when(edge)(go)

    def P1(o):
        for dp, slot in ((1, 3), (3, 1), (2, 2)):
            send((o, 0, 0), (o, 0, slot), xy(dp, 0), o)
        for ds, slot in ((1, 3), (3, 1)):
            send((o, 0, 0), (o, slot, 0), xy(0, ds), o)

    def S1(o):
        for p in (1, 3, 2):
            got((o, 0, p))
            for ds, slot in ((1, 3), (3, 1)):
                send((o, 0, p), (o, slot, p), xy(0, ds), o)

    def S2(o):
        for sl, p, ds in ((3, 0, 1), (1, 3, 3), (3, 1, 1), (1, 2, 3)):
            got((o, sl, p))
            send((o, sl, p), (o, 2, p), xy(0, ds), o)

    def F(o):
        for s in ((3, 2), (3, 3), (1, 0), (1, 1), (2, 0), (2, 1), (2, 2), (2, 3)):
            got((o,) + s)

    def zf1():
        got((1, 0, 0))
        send((1, 0, 0), (2, 0, 0), zz(pair), 1)

    def zf3():
        got((3, 0, 0))

        def go():
            remote(buf.at[3, 0, 0], buf.at[3, 0, 0], ss.at[3, 15], rs.at[3, 0, 0], zz(pair)).start()

        pl.when(edge)(go)

    def halo_copies(b):
        tiles = pl.ds(b * BATCH, BATCH)
        return (
            remote(tail.at[tiles], halo.at[tiles], hs.at[b, 0], hr.at[b, 0], after),
            remote(zs.at[tiles, pl.ds(256, LF)], zs.at[tiles, pl.ds(0, LF)], hs.at[b, 1], hr.at[b, 1], after),
        )

    def conv(ct, m, r0, rows):
        total = wt[ct, 8 * m : 8 * m + 1, :] * xt[m, r0 : r0 + rows, :]
        for j in range(1, TAPS):
            total = total + wt[ct, 8 * m + j : 8 * m + j + 1, :] * xt[m, r0 - j : r0 - j + rows, :]
        return total

    def A(b):
        load(b).wait()

        def body(ct, _):
            chans = pl.ds(pl.multiple_of(ct * C, C), C)
            for m in range(3):
                turned = jnp.transpose(xs[m, chans, :])
                tail[ct, m] = turned[T - 16 :, :]
                wide = turned.astype(F32)
                head[ct, m] = wide[:16]
                xt[m, 16 : 16 + T, :] = wide
            for r in range(0, T, 64):
                zs[ct, LF + r : LF + r + 64, :] = (conv(ct, 1, 16 + r, 64) * conv(ct, 2, 16 + r, 64)).astype(BF16)
                qs[ct, r : r + 64, :] = conv(ct, 0, 16 + r, 64)
            return 0

        lax.fori_loop(b * BATCH, (b + 1) * BATCH, body, 0)

        def go():
            for cp in halo_copies(b):
                cp.start()

        pl.when(jnp.logical_not(last))(go)

    lane = lax.broadcasted_iota(jnp.int32, (1, 256), 1)
    masks = [jnp.where((lane // 16) % 8 == g, 1.0, 0.0).astype(BF16) for g in range(8)]
    mine = pl.ds(pl.multiple_of(k * T, T), T)
    other = pl.ds(pl.multiple_of((1 - k) * T, T), T)

    def B(b):
        def come():
            for cp in halo_copies(b):
                cp.wait_recv()

        pl.when(jnp.logical_not(first))(come)

        def body(ct, _):
            for m in range(3):
                xt[m, 0:16, :] = halo[ct, m].astype(F32)
                xt[m, 16:32, :] = head[ct, m]
            zs[ct, LF : LF + 16, :] = (conv(ct, 1, 16, 16) * conv(ct, 2, 16, 16)).astype(BF16)
            qs[ct, 0:16, :] = conv(ct, 0, 16, 16)
            both = jnp.concatenate([zs[ct, 0:256, :], zs[ct, 128:384, :]], axis=1)
            total = jnp.zeros((LF, 256), F32)
            for g in range(8):
                total = total + jnp.dot(
                    toe[ct, :, 256 * g : 256 * g + 256], both * masks[g], preferred_element_type=F32
                )
            for h in range(2):
                gated = (qs[ct, 128 * h : 128 * h + 128, :] * total[:, 128 * h : 128 * h + 128]).astype(BF16)
                gs[ct, pl.ds(pl.multiple_of(k * T + 128 * h, 128), 128), :] = gated
            return 0

        lax.fori_loop(b * BATCH, (b + 1) * BATCH, body, 0)
        tiles = pl.ds(b * BATCH, BATCH)
        remote(gs.at[tiles, mine], gs.at[tiles, mine], gsend.at[b], grecv.at[b], sibling).start()

    def source(o):
        if o == 0:
            return zh
        if o == 3:
            return (zh + 2) % 4
        return (zh + 4 - pair * (3 - 2 * o)) % 4

    def out_copies(j):
        n = (y + j) % 4
        cols = pl.ds(pl.multiple_of(k * 1024 + n * 256, 256), 256)
        return (
            remote(stage.at[j, other], o_ref.at[:, cols], osend.at[j], orecv.at[j], sibling),
            pltpu.make_async_copy(stage.at[j, mine], o_ref.at[:, cols], olocal.at[j]),
        )

    def M(o):
        F(o)
        if o == 0:
            for b in range(4):
                tiles = pl.ds(b * BATCH, BATCH)
                remote(gs.at[tiles, other], gs.at[tiles, other], gsend.at[b], grecv.at[b], sibling).wait_recv()
        part = source(o) * 4
        left = jnp.concatenate([gs[part + (x + i) % 4] for i in range(4)], axis=1)
        for j in range(4):
            right = jnp.concatenate(
                [buf[o, j + (i - j) * k, i + (j - i) * k] for i in range(4)], axis=0
            )
            product = jnp.dot(left, right, preferred_element_type=F32)
            if o == 0:
                acc[j] = product
            elif o < 3:
                acc[j] += product
            else:
                stage[j] = (acc[j] + product).astype(BF16)
                for cp in out_copies(j):
                    cp.start()

    names = dict(P1=P1, S1=S1, S2=S2, A=A, B=B, M=M, zdirect=zdirect, zf1=zf1, zf3=zf3, W=lambda o: got((o, 0, 0)))
    for name, *arguments in SCHEDULE:
        names[name](*arguments)

    for cp in sent:
        cp.wait_send()

    def far_sent():
        for o, n in ((0, 13), (0, 14), (0, 15), (3, 15)):
            remote(buf.at[0, 0, 0], buf.at[0, 0, 0], ss.at[o, n], rs.at[0, 0, 0], sibling).wait_send()

    pl.when(edge)(far_sent)

    def halo_sent():
        for b in range(4):
            for cp in halo_copies(b):
                cp.wait_send()

    pl.when(jnp.logical_not(last))(halo_sent)
    for b in range(4):
        tiles = pl.ds(b * BATCH, BATCH)
        remote(gs.at[tiles, mine], gs.at[tiles, mine], gsend.at[b], grecv.at[b], sibling).wait_send()
    for j in range(4):
        there, here = out_copies(j)
        there.wait_send()
        here.wait()
    for j in range(4):
        n = (y + j) % 4
        cols = pl.ds(pl.multiple_of((1 - k) * 1024 + n * 256, 256), 256)
        remote(stage.at[j, other], o_ref.at[:, cols], osend.at[j], orecv.at[j], sibling).wait_recv()


def on_device(features, short_taps, filters, out_weight):
    dma = pltpu.SemaphoreType.DMA
    any_space = pl.BlockSpec(memory_space=pl.ANY)
    out = pl.pallas_call(
        kernel,
        out_shape=jax.ShapeDtypeStruct((T, 2048), BF16),
        in_specs=[pl.BlockSpec(memory_space=pltpu.HBM)] * 4,
        out_specs=any_space,
        scratch_shapes=[
            pltpu.VMEM((3, TAPS, 2048), BF16),
            pltpu.VMEM((LF, LF), BF16),
            pltpu.VMEM((4, 4, 4, C, 256), BF16),
            pltpu.VMEM((3, 2048, T), BF16),
            pltpu.VMEM((3, T + 16, C), F32),
            pltpu.VMEM((TILES, 24, C), F32),
            pltpu.VMEM((LF, LF), F32),
            pltpu.VMEM((TILES, LF, 8 * 256), BF16),
            pltpu.VMEM((TILES, LF + T, C), BF16),
            pltpu.VMEM((TILES, T, C), F32),
            pltpu.VMEM((TILES, 3, 16, C), F32),
            pltpu.VMEM((TILES, 3, 16, C), BF16),
            pltpu.VMEM((TILES, 3, 16, C), BF16),
            pltpu.VMEM((TILES, 2 * T, C), BF16),
            pltpu.VMEM((4, 2 * T, 256), F32),
            pltpu.VMEM((4, 2 * T, 256), BF16),
            dma((4, 17)), dma((4, 4, 4)), dma((7,)), dma((4, 2)), dma((4, 2)),
            dma((4,)), dma((4,)), dma((4,)), dma((4,)), dma((4,)),
        ],
        compiler_params=pltpu.CompilerParams(
            collective_id=0, has_side_effects=True, vmem_limit_bytes=VMEM_BYTES
        ),
        name="hyena",
    )(features, jnp.transpose(short_taps, (1, 0, 2)), filters, out_weight)
    return out[None]


def solution(mesh):
    in_specs = (P("fsdp", None, None, "ctx"), P(), P(), P("fsdp", None))
    return jax.shard_map(
        on_device, mesh=mesh, in_specs=in_specs, out_specs=P("fsdp", "ctx", None), check_vma=False
    )
```

```python
import functools

import jax
import jax.numpy as jnp
from jax import lax
from jax.experimental import pallas as pl
from jax.experimental.pallas import tpu as pltpu
from jax.sharding import PartitionSpec as P

MESH = pl.DeviceIdType.MESH
F32, BF16 = jnp.float32, jnp.bfloat16
T = 256
C = 128
TILES = 16
TAPS = 7
LF = 128
VMEM_BYTES = 56 * 1024 * 1024
BATCH = 4

SCHEDULE = (
    ("zdirect",), ("P1", 0), ("A", 0), ("S1", 0), ("zf1",), ("P1", 1), ("A", 1), ("S1", 1), ("W", 2),
    ("P1", 2), ("A", 2), ("zf3",), ("P1", 3), ("S2", 0), ("Q", 2), ("A", 3), ("S2", 1), ("S1", 2), ("Q", 0),
    ("Q", 1), ("B", 0), ("S1", 3), ("B", 1), ("S2", 2), ("B", 2), ("S2", 3), ("B", 3), ("M", 1), ("M", 0),
    ("M", 2), ("M", 3),
)


def kernel(x_ref, taps_hbm, filt_hbm, w_ref, o_ref,
           taps_ref, filt_ref, buf, xs, xt, wt, fr, toe, zs, qs, head, tail, halo, gs, acc, stage,
           ss, rs, sq, rq, lsem, hs, hr, gsend, grecv, osend, orecv, olocal):
    f = lax.axis_index("fsdp")
    c = lax.axis_index("ctx")
    zh, x = f // 4, f % 4
    zl, y, k = c // 8, (c // 2) % 4, c % 2
    z = zh * 4 + zl

    def at(x, y, z, k):
        return ((z // 4) * 4 + x, ((z % 4) * 4 + y) * 2 + k)

    def xy(dp, ds):
        return at((x + dp + (ds - dp) * k) % 4, (y + ds + (dp - ds) * k) % 4, z, k)

    def zz(d):
        return at(x, y, (z + d + 16) % 16, k)

    sibling = at(x, y, z, 1 - k)
    before, after = (f, (c + 31) % 32), (f, (c + 1) % 32)
    inner = ((zl + 1) // 2) % 2
    edge = inner == 0
    sg = (zl // 3) * 2 - 1
    pair = 1 - 2 * (zl % 2)
    srcd = -pair * (1 + 2 * inner)
    first, last = c == 0, c == 31

    def remote(src, dst, s, r, dev):
        return pltpu.make_async_remote_copy(
            src_ref=src, dst_ref=dst, send_sem=s, recv_sem=r, device_id=dev, device_id_type=MESH
        )

    barrier = pltpu.get_barrier_semaphore()

    def sig(d):
        pl.semaphore_signal(barrier, inc=1, device_id=d, device_id_type=MESH)

    for d in (xy(1, 0), xy(3, 0), xy(2, 0), xy(0, 1), xy(0, 3), zz(pair), zz(srcd), sibling):
        sig(d)
    pl.when(edge)(lambda: sig(zz(5 * sg)))
    pl.when(jnp.logical_not(first))(lambda: sig(before))

    def load(b):
        rows = pl.ds(b * BATCH * C, BATCH * C)
        return pltpu.make_async_copy(x_ref.at[0, :, rows], xs.at[:, rows], lsem.at[b])

    own = pltpu.make_async_copy(
        w_ref.at[:, pl.ds(pl.multiple_of(k * 1024 + y * 256, 256), 256)], buf.at[0, 0, 0], lsem.at[4]
    )
    small = (
        pltpu.make_async_copy(filt_hbm, filt_ref, lsem.at[5]),
        pltpu.make_async_copy(taps_hbm, taps_ref, lsem.at[6]),
    )
    own.start()
    for cp in small:
        cp.start()
    for b in range(4):
        load(b).start()
    for cp in small:
        cp.wait()

    for m in range(3):
        row = taps_ref[m].astype(F32)
        for ct in range(TILES):
            wt[ct, 8 * m : 8 * m + TAPS, :] = row[:, ct * C : (ct + 1) * C]
    r_i = lax.broadcasted_iota(jnp.int32, (LF, LF), 0)
    c_i = lax.broadcasted_iota(jnp.int32, (LF, LF), 1)
    flip = jnp.where((r_i + c_i) % LF == 0, 1.0, 0.0).astype(BF16)
    fr[...] = jnp.dot(filt_ref[...], flip, preferred_element_type=F32)

    def build(ct, _):
        rows = fr[pl.ds(pl.multiple_of(ct * 8, 8), 8), :]
        for g in range(8):
            wide = jnp.broadcast_to(rows[g : g + 1, :], (LF, LF))
            turned = pltpu.roll(wide, 0, 1, stride=1, stride_axis=0)
            toe[ct, :, 256 * g : 256 * g + 128] = jnp.where(r_i < c_i, turned, 0.0).astype(BF16)
            toe[ct, :, 256 * g + 128 : 256 * g + 256] = jnp.where(r_i >= c_i, turned, 0.0).astype(BF16)
        return 0

    lax.fori_loop(0, TILES, build, 0)
    xt[:, 0:16, :] = jnp.zeros((3, 16, C), F32)

    def empty():
        halo[...] = jnp.zeros(halo.shape, BF16)
        zs[:, 0:LF, :] = jnp.zeros((TILES, LF, C), BF16)

    pl.when(first)(empty)
    own.wait()
    pl.semaphore_wait(barrier, 7 + 3 * (1 - inner) + jnp.where(last, 0, 1))

    sent = []
    count = [0] * 4

    half = pl.ds(pl.multiple_of(zl % 2 * 64, 64), 64)
    rest = pl.ds(pl.multiple_of((1 - zl % 2) * 64, 64), 64)

    def piece(slot):
        return buf.at[(*slot, half)] if slot[0] == 0 else buf.at[slot]

    def send(src, dst, dev, o):
        cp = remote(piece(src), piece(dst), ss.at[o, count[o]], rs.at[dst], dev)
        count[o] += 1
        cp.start()
        sent.append(cp)

    def got(slot):
        remote(piece(slot), piece(slot), ss.at[0, 0], rs.at[slot], sibling).wait_recv()

    def share(s, p):
        cp = remote(buf.at[0, s, p, half], buf.at[0, s, p, half], sq.at[s, p], rq.at[s, p], zz(pair))
        cp.start()
        sent.append(cp)

    far = ((1, 1, 13), (3, 1, 14), (5, 3, 15))

    def zdirect():
        def go():
            for m, o, n in far:
                remote(buf.at[0, 0, 0], buf.at[o, 0, 0], ss.at[0, n], rs.at[o, 0, 0], zz(m * sg)).start()

        pl.when(edge)(go)

    def P1(o):
        for dp, slot in ((1, 3), (3, 1), (2, 2)):
            send((o, 0, 0), (o, 0, slot), xy(dp, 0), o)
        for ds, slot in ((1, 3), (3, 1)):
            send((o, 0, 0), (o, slot, 0), xy(0, ds), o)

    def S1(o):
        for p in (1, 3, 2):
            got((o, 0, p))
            for ds, slot in ((1, 3), (3, 1)):
                send((o, 0, p), (o, slot, p), xy(0, ds), o)

    def S2(o):
        for sl, p, ds in ((3, 0, 1), (1, 3, 3), (3, 1, 1), (1, 2, 3)):
            got((o, sl, p))
            send((o, sl, p), (o, 2, p), xy(0, ds), o)

    late = ((3, 2), (3, 3), (1, 0), (1, 1), (2, 0), (2, 1), (2, 2), (2, 3))

    def Q(some):
        if some == 2:
            for s, p in ((0, 1), (0, 3), (0, 2), (3, 0), (1, 3), (3, 1), (1, 2)):
                share(s, p)
            return
        for s, p in late[:4] if some == 0 else late[4:]:
            got((0, s, p))
            share(s, p)

    def F(o):
        if o > 0:
            for s in late:
                got((o,) + s)
            return
        for s in range(4):
            for p in range(4):
                if s or p:
                    theirs = buf.at[0, s, p, rest]
                    remote(theirs, theirs, sq.at[s, p], rq.at[s, p], sibling).wait_recv()

    def zf1():
        got((1, 0, 0))
        send((1, 0, 0), (2, 0, 0), zz(pair), 1)

    def zf3():
        got((3, 0, 0))

        def go():
            remote(buf.at[3, 0, 0], buf.at[3, 0, 0], ss.at[3, 15], rs.at[3, 0, 0], zz(pair)).start()

        pl.when(edge)(go)

    def halo_copies(b):
        tiles = pl.ds(b * BATCH, BATCH)
        return (
            remote(tail.at[tiles], halo.at[tiles], hs.at[b, 0], hr.at[b, 0], after),
            remote(zs.at[tiles, pl.ds(256, LF)], zs.at[tiles, pl.ds(0, LF)], hs.at[b, 1], hr.at[b, 1], after),
        )

    def conv(ct, m, r0, rows):
        total = wt[ct, 8 * m : 8 * m + 1, :] * xt[m, r0 : r0 + rows, :]
        for j in range(1, TAPS):
            total = total + wt[ct, 8 * m + j : 8 * m + j + 1, :] * xt[m, r0 - j : r0 - j + rows, :]
        return total

    def A(b):
        load(b).wait()

        def body(ct, _):
            chans = pl.ds(pl.multiple_of(ct * C, C), C)
            for m in range(3):
                turned = jnp.transpose(xs[m, chans, :])
                tail[ct, m] = turned[T - 16 :, :]
                wide = turned.astype(F32)
                head[ct, m] = wide[:16]
                xt[m, 16 : 16 + T, :] = wide
            for r in range(0, T, 64):
                zs[ct, LF + r : LF + r + 64, :] = (conv(ct, 1, 16 + r, 64) * conv(ct, 2, 16 + r, 64)).astype(BF16)
                qs[ct, r : r + 64, :] = conv(ct, 0, 16 + r, 64)
            return 0

        lax.fori_loop(b * BATCH, (b + 1) * BATCH, body, 0, unroll=2)

        def go():
            for cp in halo_copies(b):
                cp.start()

        pl.when(jnp.logical_not(last))(go)

    lane = lax.broadcasted_iota(jnp.int32, (1, 256), 1)
    masks = [jnp.where((lane // 16) % 8 == g, 1.0, 0.0).astype(BF16) for g in range(8)]
    mine = pl.ds(pl.multiple_of(k * T, T), T)
    other = pl.ds(pl.multiple_of((1 - k) * T, T), T)

    def B(b):
        def come():
            for cp in halo_copies(b):
                cp.wait_recv()

        pl.when(jnp.logical_not(first))(come)

        def body(ct, _):
            for m in range(3):
                xt[m, 0:16, :] = halo[ct, m].astype(F32)
                xt[m, 16:32, :] = head[ct, m]
            zs[ct, LF : LF + 16, :] = (conv(ct, 1, 16, 16) * conv(ct, 2, 16, 16)).astype(BF16)
            qs[ct, 0:16, :] = conv(ct, 0, 16, 16)
            both = jnp.concatenate([zs[ct, 0:256, :], zs[ct, 128:384, :]], axis=1)
            total = jnp.zeros((LF, 256), F32)
            for g in range(8):
                total = total + jnp.dot(
                    toe[ct, :, 256 * g : 256 * g + 256], both * masks[g], preferred_element_type=F32
                )
            for h in range(2):
                gated = (qs[ct, 128 * h : 128 * h + 128, :] * total[:, 128 * h : 128 * h + 128]).astype(BF16)
                gs[ct, pl.ds(pl.multiple_of(k * T + 128 * h, 128), 128), :] = gated
            return 0

        lax.fori_loop(b * BATCH, (b + 1) * BATCH, body, 0, unroll=2)
        tiles = pl.ds(b * BATCH, BATCH)
        remote(gs.at[tiles, mine], gs.at[tiles, mine], gsend.at[b], grecv.at[b], sibling).start()

    def source(o):
        if o == 0:
            return zh
        if o == 3:
            return (zh + 2) % 4
        return (zh + 4 - pair * (3 - 2 * o)) % 4

    def out_copies(j):
        n = (y + j) % 4
        cols = pl.ds(pl.multiple_of(k * 1024 + n * 256, 256), 256)
        return (
            remote(stage.at[j, other], o_ref.at[:, cols], osend.at[j], orecv.at[j], sibling),
            pltpu.make_async_copy(stage.at[j, mine], o_ref.at[:, cols], olocal.at[j]),
        )

    def M(o):
        F(o)
        if o == 1:
            for b in range(4):
                tiles = pl.ds(b * BATCH, BATCH)
                remote(gs.at[tiles, other], gs.at[tiles, other], gsend.at[b], grecv.at[b], sibling).wait_recv()
        part = source(o) * 4
        left = jnp.concatenate([gs[part + (x + i) % 4] for i in range(4)], axis=1)
        for j in range(4):
            right = jnp.concatenate(
                [buf[o, j + (i - j) * k, i + (j - i) * k] for i in range(4)], axis=0
            )
            product = jnp.dot(left, right, preferred_element_type=F32)
            if o == 1:
                acc[j] = product
            elif o < 3:
                acc[j] += product
            else:
                stage[j] = (acc[j] + product).astype(BF16)
                for cp in out_copies(j):
                    cp.start()

    names = dict(Q=Q, P1=P1, S1=S1, S2=S2, A=A, B=B, M=M, zdirect=zdirect, zf1=zf1, zf3=zf3, W=lambda o: got((o, 0, 0)))
    for name, *arguments in SCHEDULE:
        names[name](*arguments)

    for cp in sent:
        cp.wait_send()

    def far_sent():
        for o, n in ((0, 13), (0, 14), (0, 15), (3, 15)):
            remote(buf.at[0, 0, 0], buf.at[0, 0, 0], ss.at[o, n], rs.at[0, 0, 0], sibling).wait_send()

    pl.when(edge)(far_sent)

    def halo_sent():
        for b in range(4):
            for cp in halo_copies(b):
                cp.wait_send()

    pl.when(jnp.logical_not(last))(halo_sent)
    for b in range(4):
        tiles = pl.ds(b * BATCH, BATCH)
        remote(gs.at[tiles, mine], gs.at[tiles, mine], gsend.at[b], grecv.at[b], sibling).wait_send()
    for j in range(4):
        there, here = out_copies(j)
        there.wait_send()
        here.wait()
    for j in range(4):
        n = (y + j) % 4
        cols = pl.ds(pl.multiple_of((1 - k) * 1024 + n * 256, 256), 256)
        remote(stage.at[j, other], o_ref.at[:, cols], osend.at[j], orecv.at[j], sibling).wait_recv()


def on_device(features, short_taps, filters, out_weight):
    dma = pltpu.SemaphoreType.DMA
    any_space = pl.BlockSpec(memory_space=pl.ANY)
    out = pl.pallas_call(
        kernel,
        out_shape=jax.ShapeDtypeStruct((T, 2048), BF16),
        in_specs=[pl.BlockSpec(memory_space=pltpu.HBM)] * 4,
        out_specs=any_space,
        scratch_shapes=[
            pltpu.VMEM((3, TAPS, 2048), BF16),
            pltpu.VMEM((LF, LF), BF16),
            pltpu.VMEM((4, 4, 4, C, 256), BF16),
            pltpu.VMEM((3, 2048, T), BF16),
            pltpu.VMEM((3, T + 16, C), F32),
            pltpu.VMEM((TILES, 24, C), F32),
            pltpu.VMEM((LF, LF), F32),
            pltpu.VMEM((TILES, LF, 8 * 256), BF16),
            pltpu.VMEM((TILES, LF + T, C), BF16),
            pltpu.VMEM((TILES, T, C), F32),
            pltpu.VMEM((TILES, 3, 16, C), F32),
            pltpu.VMEM((TILES, 3, 16, C), BF16),
            pltpu.VMEM((TILES, 3, 16, C), BF16),
            pltpu.VMEM((TILES, 2 * T, C), BF16),
            pltpu.VMEM((4, 2 * T, 256), F32),
            pltpu.VMEM((4, 2 * T, 256), BF16),
            dma((4, 17)), dma((4, 4, 4)), dma((4, 4)), dma((4, 4)), dma((7,)), dma((4, 2)), dma((4, 2)),
            dma((4,)), dma((4,)), dma((4,)), dma((4,)), dma((4,)),
        ],
        compiler_params=pltpu.CompilerParams(
            collective_id=0, has_side_effects=True, vmem_limit_bytes=VMEM_BYTES
        ),
        name="hyena",
    )(features, jnp.transpose(short_taps, (1, 0, 2)), filters, out_weight)
    return out[None]


def solution(mesh):
    in_specs = (P("fsdp", None, None, "ctx"), P(), P(), P("fsdp", None))
    return jax.shard_map(
        on_device, mesh=mesh, in_specs=in_specs, out_specs=P("fsdp", "ctx", None), check_vma=False
    )
```

```python
import functools

import jax
import jax.numpy as jnp
from jax import lax
from jax.experimental import pallas as pl
from jax.experimental.pallas import tpu as pltpu
from jax.sharding import PartitionSpec as P

MESH = pl.DeviceIdType.MESH
F32, BF16 = jnp.float32, jnp.bfloat16
T = 256
C = 128
TILES = 16
TAPS = 7
LF = 128
VMEM_BYTES = 56 * 1024 * 1024
BATCH = 4

SCHEDULE = (
    ("zdirect",), ("P1", 0), ("A", 0), ("S1", 0), ("zf1",), ("P1", 1), ("A", 1), ("S1", 1), ("A", 2),
    ("W", 2), ("P1", 2), ("zf3",), ("P1", 3), ("S2", 0), ("Q", 2), ("A", 3), ("S2", 1), ("S1", 2), ("Q", 0),
    ("Q", 1), ("B", 0), ("S1", 3), ("B", 1), ("S2", 2), ("B", 2), ("S2", 3), ("B", 3), ("M", 1), ("M", 0),
    ("M", 2), ("M", 3),
)


def kernel(x_ref, taps_hbm, filt_hbm, w_ref, o_ref,
           taps_ref, filt_ref, buf, xs, xt, wt, fr, toe, zs, qs, head, tail, halo, gs, acc, stage,
           ss, rs, sq, rq, lsem, hs, hr, gsend, grecv, osend, orecv, olocal):
    f = lax.axis_index("fsdp")
    c = lax.axis_index("ctx")
    zh, x = f // 4, f % 4
    zl, y, k = c // 8, (c // 2) % 4, c % 2
    z = zh * 4 + zl

    def at(x, y, z, k):
        return ((z // 4) * 4 + x, ((z % 4) * 4 + y) * 2 + k)

    def xy(dp, ds):
        return at((x + dp + (ds - dp) * k) % 4, (y + ds + (dp - ds) * k) % 4, z, k)

    def zz(d):
        return at(x, y, (z + d + 16) % 16, k)

    sibling = at(x, y, z, 1 - k)
    before, after = (f, (c + 31) % 32), (f, (c + 1) % 32)
    inner = ((zl + 1) // 2) % 2
    edge = inner == 0
    sg = (zl // 3) * 2 - 1
    pair = 1 - 2 * (zl % 2)
    srcd = -pair * (1 + 2 * inner)
    first, last = c == 0, c == 31

    def remote(src, dst, s, r, dev):
        return pltpu.make_async_remote_copy(
            src_ref=src, dst_ref=dst, send_sem=s, recv_sem=r, device_id=dev, device_id_type=MESH
        )

    barrier = pltpu.get_barrier_semaphore()

    def sig(d):
        pl.semaphore_signal(barrier, inc=1, device_id=d, device_id_type=MESH)

    for d in (xy(1, 0), xy(3, 0), xy(2, 0), xy(0, 1), xy(0, 3), zz(pair), zz(srcd), sibling):
        sig(d)
    pl.when(edge)(lambda: sig(zz(5 * sg)))
    pl.when(jnp.logical_not(first))(lambda: sig(before))

    def load(b):
        rows = pl.ds(b * BATCH * C, BATCH * C)
        return pltpu.make_async_copy(x_ref.at[0, :, rows], xs.at[:, rows], lsem.at[b])

    own = pltpu.make_async_copy(
        w_ref.at[:, pl.ds(pl.multiple_of(k * 1024 + y * 256, 256), 256)], buf.at[0, 0, 0], lsem.at[4]
    )
    small = (
        pltpu.make_async_copy(filt_hbm, filt_ref, lsem.at[5]),
        pltpu.make_async_copy(taps_hbm, taps_ref, lsem.at[6]),
    )
    own.start()
    for cp in small:
        cp.start()
    for b in range(4):
        load(b).start()
    for cp in small:
        cp.wait()

    for m in range(3):
        row = taps_ref[m].astype(F32)
        for ct in range(TILES):
            wt[ct, 8 * m : 8 * m + TAPS, :] = row[:, ct * C : (ct + 1) * C]
    r_i = lax.broadcasted_iota(jnp.int32, (LF, LF), 0)
    c_i = lax.broadcasted_iota(jnp.int32, (LF, LF), 1)
    flip = jnp.where((r_i + c_i) % LF == 0, 1.0, 0.0).astype(BF16)
    fr[...] = jnp.dot(filt_ref[...], flip, preferred_element_type=F32)

    def build(ct, _):
        rows = fr[pl.ds(pl.multiple_of(ct * 8, 8), 8), :]
        for g in range(8):
            wide = jnp.broadcast_to(rows[g : g + 1, :], (LF, LF))
            turned = pltpu.roll(wide, 0, 1, stride=1, stride_axis=0)
            toe[ct, :, 256 * g : 256 * g + 128] = jnp.where(r_i < c_i, turned, 0.0).astype(BF16)
            toe[ct, :, 256 * g + 128 : 256 * g + 256] = jnp.where(r_i >= c_i, turned, 0.0).astype(BF16)
        return 0

    lax.fori_loop(0, TILES, build, 0)
    xt[:, 0:16, :] = jnp.zeros((3, 16, C), F32)

    def empty():
        halo[...] = jnp.zeros(halo.shape, BF16)
        zs[:, 0:LF, :] = jnp.zeros((TILES, LF, C), BF16)

    pl.when(first)(empty)
    own.wait()
    pl.semaphore_wait(barrier, 7 + 3 * (1 - inner) + jnp.where(last, 0, 1))

    sent = []
    count = [0] * 4

    half = pl.ds(pl.multiple_of(zl % 2 * 64, 64), 64)
    rest = pl.ds(pl.multiple_of((1 - zl % 2) * 64, 64), 64)

    def piece(slot):
        return buf.at[(*slot, half)] if slot[0] == 0 else buf.at[slot]

    def send(src, dst, dev, o):
        cp = remote(piece(src), piece(dst), ss.at[o, count[o]], rs.at[dst], dev)
        count[o] += 1
        cp.start()
        sent.append(cp)

    def got(slot):
        remote(piece(slot), piece(slot), ss.at[0, 0], rs.at[slot], sibling).wait_recv()

    def share(s, p):
        cp = remote(buf.at[0, s, p, half], buf.at[0, s, p, half], sq.at[s, p], rq.at[s, p], zz(pair))
        cp.start()
        sent.append(cp)

    far = ((1, 1, 13), (3, 1, 14), (5, 3, 15))

    def zdirect():
        def go():
            for m, o, n in far:
                remote(buf.at[0, 0, 0], buf.at[o, 0, 0], ss.at[0, n], rs.at[o, 0, 0], zz(m * sg)).start()

        pl.when(edge)(go)

    def P1(o):
        for dp, slot in ((1, 3), (3, 1), (2, 2)):
            send((o, 0, 0), (o, 0, slot), xy(dp, 0), o)
        for ds, slot in ((1, 3), (3, 1)):
            send((o, 0, 0), (o, slot, 0), xy(0, ds), o)

    def S1(o):
        for p in (1, 3, 2):
            got((o, 0, p))
            for ds, slot in ((1, 3), (3, 1)):
                send((o, 0, p), (o, slot, p), xy(0, ds), o)

    def S2(o):
        for sl, p, ds in ((3, 0, 1), (1, 3, 3), (3, 1, 1), (1, 2, 3)):
            got((o, sl, p))
            send((o, sl, p), (o, 2, p), xy(0, ds), o)

    late = ((3, 2), (3, 3), (1, 0), (1, 1), (2, 0), (2, 1), (2, 2), (2, 3))

    def Q(some):
        if some == 2:
            for s, p in ((0, 1), (0, 3), (0, 2), (3, 0), (1, 3), (3, 1), (1, 2)):
                share(s, p)
            return
        for s, p in late[:4] if some == 0 else late[4:]:
            got((0, s, p))
            share(s, p)

    def F(o):
        if o > 0:
            for s in late:
                got((o,) + s)
            return
        for s in range(4):
            for p in range(4):
                if s or p:
                    theirs = buf.at[0, s, p, rest]
                    remote(theirs, theirs, sq.at[s, p], rq.at[s, p], sibling).wait_recv()

    def zf1():
        got((1, 0, 0))
        send((1, 0, 0), (2, 0, 0), zz(pair), 1)

    def zf3():
        got((3, 0, 0))

        def go():
            remote(buf.at[3, 0, 0], buf.at[3, 0, 0], ss.at[3, 15], rs.at[3, 0, 0], zz(pair)).start()

        pl.when(edge)(go)

    def halo_copies(b):
        tiles = pl.ds(b * BATCH, BATCH)
        return (
            remote(tail.at[tiles], halo.at[tiles], hs.at[b, 0], hr.at[b, 0], after),
            remote(zs.at[tiles, pl.ds(256, LF)], zs.at[tiles, pl.ds(0, LF)], hs.at[b, 1], hr.at[b, 1], after),
        )

    def conv(ct, m, r0, rows):
        total = wt[ct, 8 * m : 8 * m + 1, :] * xt[m, r0 : r0 + rows, :]
        for j in range(1, TAPS):
            total = total + wt[ct, 8 * m + j : 8 * m + j + 1, :] * xt[m, r0 - j : r0 - j + rows, :]
        return total

    def A(b):
        load(b).wait()

        def body(ct, _):
            chans = pl.ds(pl.multiple_of(ct * C, C), C)
            for m in range(3):
                turned = jnp.transpose(xs[m, chans, :])
                tail[ct, m] = turned[T - 16 :, :]
                wide = turned.astype(F32)
                head[ct, m] = wide[:16]
                xt[m, 16 : 16 + T, :] = wide
            for r in range(0, T, 64):
                zs[ct, LF + r : LF + r + 64, :] = (conv(ct, 1, 16 + r, 64) * conv(ct, 2, 16 + r, 64)).astype(BF16)
                qs[ct, r : r + 64, :] = conv(ct, 0, 16 + r, 64)
            return 0

        lax.fori_loop(b * BATCH, (b + 1) * BATCH, body, 0, unroll=2)

        def go():
            for cp in halo_copies(b):
                cp.start()

        pl.when(jnp.logical_not(last))(go)

    lane = lax.broadcasted_iota(jnp.int32, (1, 256), 1)
    masks = [jnp.where((lane // 16) % 8 == g, 1.0, 0.0).astype(BF16) for g in range(8)]
    mine = pl.ds(pl.multiple_of(k * T, T), T)
    other = pl.ds(pl.multiple_of((1 - k) * T, T), T)

    def B(b):
        def come():
            for cp in halo_copies(b):
                cp.wait_recv()

        pl.when(jnp.logical_not(first))(come)

        def body(ct, _):
            for m in range(3):
                xt[m, 0:16, :] = halo[ct, m].astype(F32)
                xt[m, 16:32, :] = head[ct, m]
            zs[ct, LF : LF + 16, :] = (conv(ct, 1, 16, 16) * conv(ct, 2, 16, 16)).astype(BF16)
            qs[ct, 0:16, :] = conv(ct, 0, 16, 16)
            both = jnp.concatenate([zs[ct, 0:256, :], zs[ct, 128:384, :]], axis=1)
            total = jnp.zeros((LF, 256), F32)
            for g in range(8):
                total = total + jnp.dot(
                    toe[ct, :, 256 * g : 256 * g + 256], both * masks[g], preferred_element_type=F32
                )
            for h in range(2):
                gated = (qs[ct, 128 * h : 128 * h + 128, :] * total[:, 128 * h : 128 * h + 128]).astype(BF16)
                gs[ct, pl.ds(pl.multiple_of(k * T + 128 * h, 128), 128), :] = gated
            return 0

        lax.fori_loop(b * BATCH, (b + 1) * BATCH, body, 0, unroll=2)
        tiles = pl.ds(b * BATCH, BATCH)
        remote(gs.at[tiles, mine], gs.at[tiles, mine], gsend.at[b], grecv.at[b], sibling).start()

    def source(o):
        if o == 0:
            return zh
        if o == 3:
            return (zh + 2) % 4
        return (zh + 4 - pair * (3 - 2 * o)) % 4

    def out_copies(j):
        n = (y + j) % 4
        cols = pl.ds(pl.multiple_of(k * 1024 + n * 256, 256), 256)
        return (
            remote(stage.at[j, other], o_ref.at[:, cols], osend.at[j], orecv.at[j], sibling),
            pltpu.make_async_copy(stage.at[j, mine], o_ref.at[:, cols], olocal.at[j]),
        )

    def M(o):
        F(o)
        if o == 1:
            for b in range(4):
                tiles = pl.ds(b * BATCH, BATCH)
                remote(gs.at[tiles, other], gs.at[tiles, other], gsend.at[b], grecv.at[b], sibling).wait_recv()
        part = source(o) * 4
        left = jnp.concatenate([gs[part + (x + i) % 4] for i in range(4)], axis=1)
        for j in range(4):
            right = jnp.concatenate(
                [buf[o, j + (i - j) * k, i + (j - i) * k] for i in range(4)], axis=0
            )
            product = jnp.dot(left, right, preferred_element_type=F32)
            if o == 1:
                acc[j] = product
            elif o < 3:
                acc[j] += product
            else:
                stage[j] = (acc[j] + product).astype(BF16)
                for cp in out_copies(j):
                    cp.start()

    names = dict(Q=Q, P1=P1, S1=S1, S2=S2, A=A, B=B, M=M, zdirect=zdirect, zf1=zf1, zf3=zf3, W=lambda o: got((o, 0, 0)))
    for name, *arguments in SCHEDULE:
        names[name](*arguments)

    for cp in sent:
        cp.wait_send()

    def far_sent():
        for o, n in ((0, 13), (0, 14), (0, 15), (3, 15)):
            remote(buf.at[0, 0, 0], buf.at[0, 0, 0], ss.at[o, n], rs.at[0, 0, 0], sibling).wait_send()

    pl.when(edge)(far_sent)

    def halo_sent():
        for b in range(4):
            for cp in halo_copies(b):
                cp.wait_send()

    pl.when(jnp.logical_not(last))(halo_sent)
    for b in range(4):
        tiles = pl.ds(b * BATCH, BATCH)
        remote(gs.at[tiles, mine], gs.at[tiles, mine], gsend.at[b], grecv.at[b], sibling).wait_send()
    for j in range(4):
        there, here = out_copies(j)
        there.wait_send()
        here.wait()
    for j in range(4):
        n = (y + j) % 4
        cols = pl.ds(pl.multiple_of((1 - k) * 1024 + n * 256, 256), 256)
        remote(stage.at[j, other], o_ref.at[:, cols], osend.at[j], orecv.at[j], sibling).wait_recv()


def on_device(features, short_taps, filters, out_weight):
    dma = pltpu.SemaphoreType.DMA
    any_space = pl.BlockSpec(memory_space=pl.ANY)
    out = pl.pallas_call(
        kernel,
        out_shape=jax.ShapeDtypeStruct((T, 2048), BF16),
        in_specs=[pl.BlockSpec(memory_space=pltpu.HBM)] * 4,
        out_specs=any_space,
        scratch_shapes=[
            pltpu.VMEM((3, TAPS, 2048), BF16),
            pltpu.VMEM((LF, LF), BF16),
            pltpu.VMEM((4, 4, 4, C, 256), BF16),
            pltpu.VMEM((3, 2048, T), BF16),
            pltpu.VMEM((3, T + 16, C), F32),
            pltpu.VMEM((TILES, 24, C), F32),
            pltpu.VMEM((LF, LF), F32),
            pltpu.VMEM((TILES, LF, 8 * 256), BF16),
            pltpu.VMEM((TILES, LF + T, C), BF16),
            pltpu.VMEM((TILES, T, C), F32),
            pltpu.VMEM((TILES, 3, 16, C), F32),
            pltpu.VMEM((TILES, 3, 16, C), BF16),
            pltpu.VMEM((TILES, 3, 16, C), BF16),
            pltpu.VMEM((TILES, 2 * T, C), BF16),
            pltpu.VMEM((4, 2 * T, 256), F32),
            pltpu.VMEM((4, 2 * T, 256), BF16),
            dma((4, 17)), dma((4, 4, 4)), dma((4, 4)), dma((4, 4)), dma((7,)), dma((4, 2)), dma((4, 2)),
            dma((4,)), dma((4,)), dma((4,)), dma((4,)), dma((4,)),
        ],
        compiler_params=pltpu.CompilerParams(
            collective_id=0, has_side_effects=True, vmem_limit_bytes=VMEM_BYTES
        ),
        name="hyena",
    )(features, jnp.transpose(short_taps, (1, 0, 2)), filters, out_weight)
    return out[None]


def solution(mesh):
    in_specs = (P("fsdp", None, None, "ctx"), P(), P(), P("fsdp", None))
    return jax.shard_map(
        on_device, mesh=mesh, in_specs=in_specs, out_specs=P("fsdp", "ctx", None), check_vma=False
    )
```
